256 devices in a mesh: fsdp: 8 (over y, z_hi), replica: 32 (over x, z_lo, core).
Axes of the slice: x: 4, y: 4, z: 8 (z_hi: 2, z_lo: 4; z = z_hi * 4 + z_lo), core: 2. Of those that a mesh axis runs over, the one named last changes fastest.
Arguments:
- params: bfloat16 [32, 8, 2048, 512], P('replica', None, 'fsdp'), may hold values from -2.390625 to 2.390625
- momentum: bfloat16 [32, 8, 2048, 512], P('replica', None, 'fsdp'), may hold values from -6 to 6
- grads: bfloat16 [2, 32, 8, 2048, 512], P(None, 'replica', None, 'fsdp'), may hold values from -6 to 6
Outputs:
- new_params: bfloat16 [32, 8, 2048, 512], P('replica', None, 'fsdp')
- new_momentum: bfloat16 [32, 8, 2048, 512], P('replica', None, 'fsdp')
The draws below stay inside these ranges and needn't reach their ends.
All inputs are finite; a program needn't handle non-finite values.
Results may differ from the reference program's by a relative error of at most 0.013.
Values may be sent and summed in bfloat16 or wider, within the bound.
No kernel may reach another device: no remote copies, remote signals or barrier semaphores. Data moves between devices by JAX's collectives and lax.ppermute only.
A program may use at most 128 MiB of HBM per device.

```python
import math
import jax
import jax.numpy as jnp
from jax import lax

ROWS = 2048
COLS = 512
NS_ITERS = 3
STEPS = 2
MATRICES = 8
REPLICAS = 32


def shard_levels(own_key, dims, shards, low, high):
    def one(position, blocks):
        draws = jax.random.uniform(jax.random.fold_in(jax.random.fold_in(own_key, 6), position), (blocks,), jnp.float32, low / len(shards), high / len(shards))
        return jnp.repeat(jnp.exp(draws), dims[position] // blocks).reshape((-1,) + (1,) * (len(dims) - position - 1))

    gain = one(*shards[0])
    for cut in shards[1:]:
        gain = gain * one(*cut)
    return gain


def normal_values(own_key, dims, width, limit, cuts=(), dtype=jnp.bfloat16):
    loudness = shard_levels(own_key, dims, cuts, -0.22, 0.18) if cuts else 1.0
    drawn = jax.random.normal(own_key, dims, jnp.float32) * width * loudness
    return jnp.minimum(jnp.maximum(drawn, -limit), limit).astype(dtype)


def setup_inputs(seed: int = 0) -> dict:
    splits = jax.random.split(jax.random.key(seed), 4)
    return {
        "params": normal_values(splits[0], (REPLICAS, MATRICES, ROWS, COLS), 0.3, 2.390625, ((0, 32), (2, 8))),
        "momentum": normal_values(splits[1], (REPLICAS, MATRICES, ROWS, COLS), 1.0, 6.0, ((0, 32), (2, 8))),
        "grads": normal_values(splits[2], (STEPS, REPLICAS, MATRICES, ROWS, COLS), 1.0, 6.0, ((1, 32), (3, 8))),
    }


BETA = 0.95
LEARN = 0.5
COEF_A = 3.4445
COEF_B = -4.775
COEF_C = 2.0315

def newton_schulz(matrix):
    xf = matrix.astype(jnp.float32)
    total = jnp.sqrt(jnp.sum(xf * xf))
    ycur = (xf / (total + 1e-07)).astype(jnp.bfloat16)
    for _ in range(NS_ITERS):
        gram = lax.dot_general(ycur, ycur, (((0,), (0,)), ((), ())), preferred_element_type=jnp.float32).astype(jnp.bfloat16)
        square = jnp.dot(gram, gram, preferred_element_type=jnp.float32)
        poly = (COEF_B * gram.astype(jnp.float32) + COEF_C * square).astype(jnp.bfloat16)
        ycur = (COEF_A * ycur.astype(jnp.float32) + jnp.dot(ycur, poly, preferred_element_type=jnp.float32)).astype(jnp.bfloat16)
    return ycur

def partner(values, span):
    shape = values.shape
    folded = values.reshape((shape[0] // (2 * span), 2, span) + shape[1:])
    return folded[:, ::-1].reshape(shape)

def reference(params, momentum, grads):
    step_scale = LEARN * 0.2 * math.sqrt(max(ROWS, COLS))
    pcur = params
    mcur = momentum
    for step in range(STEPS):
        grad = grads[step].astype(jnp.float32)
        m_new = (BETA * mcur.astype(jnp.float32) + grad).astype(jnp.bfloat16)
        nest = (grad + BETA * m_new.astype(jnp.float32)).astype(jnp.bfloat16)
        flat = nest.reshape(-1, ROWS, COLS)
        update = lax.map(newton_schulz, flat).reshape(nest.shape)
        local = (pcur.astype(jnp.float32) - step_scale * update.astype(jnp.float32)).astype(jnp.bfloat16)
        span = 2 ** step
        lfloat = local.astype(jnp.float32)
        pcur = (0.5 * (lfloat + partner(lfloat, span))).astype(jnp.bfloat16)
        mfloat = m_new.astype(jnp.float32)
        mcur = (0.5 * (mfloat + partner(mfloat, span))).astype(jnp.bfloat16)
    return (pcur, mcur)
```

```python
import functools
import math

import jax
import jax.numpy as jnp
from jax import lax
from jax.experimental import pallas as pl
from jax.experimental.pallas import tpu as pltpu
from jax.sharding import PartitionSpec as P

ROWS = 2048
COLS = 512
HALF = COLS // 2
PART = 256
MATS = 8
NS_ITERS = 3
STEPS = 2
PACKED = COLS + 16

BETA = 0.95
LEARN = 0.5
COEF_A = 3.4445
COEF_B = -4.775
COEF_C = 2.0315
SCALE = LEARN * 0.2 * math.sqrt(max(ROWS, COLS))

F32 = jnp.float32
BF16 = jnp.bfloat16
PAIR = jax.ShapeDtypeStruct((2, PART, COLS), BF16)
WHOLE = jax.ShapeDtypeStruct((MATS, PART, COLS), BF16)
BLOCK = (1, PART, COLS)
MIB = 1 << 20


def mat_of(step, y_ref):
    return (step % 2) * 4 + (y_ref[0] + step // 2) % 4


def natural(step, y_ref):
    return (mat_of(step, y_ref), 0, 0)


def group_spec(place):
    return pl.BlockSpec(BLOCK, lambda t, y_ref: (jnp.clip(t - 2 * place, 0, 1), 0, 0))


def params_of(mib):
    return pltpu.CompilerParams(vmem_limit_bytes=mib * MIB)


def cost(flops, nbytes):
    return pl.CostEstimate(flops=flops, bytes_accessed=nbytes, transcendentals=0)


def first_kernel(y_ref, m_ref, g_ref, new_ref, *nest_refs):
    t = pl.program_id(0)
    grad = g_ref[0, 0, 0].astype(F32)
    m_new = (BETA * m_ref[0].astype(F32) + grad).astype(BF16)
    new_ref[0] = m_new
    nest = (grad + BETA * m_new.astype(F32)).astype(BF16)
    for d in range(4):
        @pl.when(t // 2 == d)
        def _():
            nest_refs[d][0] = nest


def first_step(y, momentum, grads):
    return pl.pallas_call(
        first_kernel,
        grid_spec=pltpu.PrefetchScalarGridSpec(
            num_scalar_prefetch=1,
            grid=(MATS,),
            in_specs=[
                pl.BlockSpec(BLOCK, natural),
                pl.BlockSpec((1, 1, 1, PART, COLS), lambda t, y_ref: (0, 0, mat_of(t, y_ref), 0, 0)),
            ],
            out_specs=[pl.BlockSpec(BLOCK, natural)] + [group_spec(d) for d in range(4)],
        ),
        out_shape=[WHOLE] + [PAIR] * 4,
        compiler_params=params_of(16),
        cost_estimate=cost(10 * MIB, 8 * MIB),
        name="nest_first",
    )(y, momentum, grads)


def second_kernel(y_ref, m_ref, peer_ref, g_ref, *out_refs):
    t = pl.program_id(0)
    grad = g_ref[0, 0, 0].astype(F32)
    mean = (0.5 * (m_ref[0].astype(F32) + peer_ref[0].astype(F32))).astype(BF16)
    m_new = (BETA * mean.astype(F32) + grad).astype(BF16)
    nest = (grad + BETA * m_new.astype(F32)).astype(BF16)
    for d in range(4):
        @pl.when(t // 2 == d)
        def _():
            out_refs[d][0] = m_new
            out_refs[4 + d][0] = nest


def second_step(y, m_new, m_peer, grads):
    return pl.pallas_call(
        second_kernel,
        grid_spec=pltpu.PrefetchScalarGridSpec(
            num_scalar_prefetch=1,
            grid=(MATS,),
            in_specs=[
                pl.BlockSpec(BLOCK, natural),
                pl.BlockSpec(BLOCK, natural),
                pl.BlockSpec((1, 1, 1, PART, COLS), lambda t, y_ref: (1, 0, mat_of(t, y_ref), 0, 0)),
            ],
            out_specs=[group_spec(d) for d in range(4)] * 2,
        ),
        out_shape=[PAIR] * 8,
        compiler_params=params_of(16),
        cost_estimate=cost(10 * MIB, 10 * MIB),
        name="nest_second",
    )(y, m_new, m_peer, grads)


def iota(axis, shape=(HALF, HALF)):
    return lax.broadcasted_iota(jnp.int32, shape, axis)


def gram_kernel(*refs):
    blocks, out_ref = refs[:4], refs[4]
    left = [ref[0, :, :HALF] for ref in blocks]
    right = [ref[0, :, HALF:] for ref in blocks]

    def product(lhs, rhs):
        total = None
        for one, two in zip(lhs, rhs):
            term = lax.dot_general(one, two, (((0,), (0,)), ((), ())), preferred_element_type=F32)
            total = term if total is None else total + term
        return total

    out_ref[0, :HALF] = product(left, right).astype(BF16)
    top = product(left, left)
    low = product(right, right)
    out_ref[0, HALF:COLS] = jnp.where(iota(1) >= iota(0), top, low).astype(BF16)
    diagonal = jnp.sum(jnp.where(iota(1) == iota(0), low, 0.0), axis=0, keepdims=True)
    out_ref[0, COLS:] = jnp.broadcast_to(diagonal, (PACKED - COLS, HALF)).astype(BF16)


def gram(blocks):
    return pl.pallas_call(
        gram_kernel,
        grid=(2,),
        in_specs=[pl.BlockSpec(BLOCK, lambda k: (k, 0, 0))] * 4,
        out_specs=pl.BlockSpec((1, PACKED, HALF), lambda k: (k, 0, 0)),
        out_shape=jax.ShapeDtypeStruct((2, PACKED, HALF), BF16),
        compiler_params=params_of(16),
        cost_estimate=cost(2 * 2 * 4 * PART * COLS * COLS, 3 * MIB),
        name="partial_gram",
    )(*blocks)


def dot(lhs, rhs):
    return jnp.dot(lhs, rhs, preferred_element_type=F32)


def update_kernel(last, *refs):
    own_ref, peer_ref = refs[:2]
    x_refs = refs[2:6]
    if last:
        u_refs, v_refs = refs[6:10], refs[10:14]
        out_refs = refs[14:18]
        rest = refs[18:]
    else:
        out_refs = refs[6:10]
        rest = refs[10:]
    g_ref, gb_ref, r_ref, y_ref = rest
    inverse = []
    for k in range(2):
        packed = own_ref[k].astype(F32) + peer_ref[k].astype(F32)
        cross = packed[:HALF]
        mixed = packed[HALF:COLS]
        flipped = mixed.T
        top = jnp.where(iota(1) >= iota(0), mixed, flipped)
        low = jnp.where(iota(1) < iota(0), mixed, flipped)
        low = jnp.where(iota(1) == iota(0), packed[COLS : COLS + 1], low)
        diagonal = jnp.sum(jnp.where(iota(1) == iota(0), top, 0.0), axis=0, keepdims=True)
        diagonal += packed[COLS : COLS + 1]
        trace = jnp.sum(diagonal, axis=1, keepdims=True)
        inv = 1.0 / (jnp.sqrt(trace) + 1e-07)
        inverse.append(inv)
        g_ref[k, :HALF, :HALF] = top * inv * inv
        g_ref[k, :HALF, HALF:] = cross * inv * inv
        g_ref[k, HALF:, :HALF] = cross.T * inv * inv
        g_ref[k, HALF:, HALF:] = low * inv * inv
        gb_ref[k] = g_ref[k].astype(BF16)
    for d in range(4):
        for k in range(2):
            y_ref[k, d * PART : (d + 1) * PART] = (x_refs[d][k].astype(F32) * inverse[k]).astype(BF16)
    for step in range(NS_ITERS):
        for k in range(2):
            value = COEF_B * g_ref[k] + COEF_C * dot(gb_ref[k], gb_ref[k])
            r_ref[k] = value.astype(BF16)
        if step < NS_ITERS - 1:
            for k in range(2):
                value = COEF_A * g_ref[k] + dot(gb_ref[k], r_ref[k])
                g_ref[k] = value
                gb_ref[k] = value.astype(BF16)
            for k in range(2):
                value = COEF_A * g_ref[k] + dot(gb_ref[k], r_ref[k])
                g_ref[k] = value
                gb_ref[k] = value.astype(BF16)
        for d in range(4):
            for k in range(2):
                block = y_ref[k, d * PART : (d + 1) * PART]
                value = COEF_A * block.astype(F32) + dot(block, r_ref[k])
                if step < NS_ITERS - 1:
                    y_ref[k, d * PART : (d + 1) * PART] = value.astype(BF16)
                elif last:
                    mean = 0.5 * (u_refs[d][k].astype(F32) + v_refs[d][k].astype(F32))
                    out_refs[d][k] = (value + mean).astype(BF16)
                else:
                    out_refs[d][k] = value.astype(BF16)


def update(own, peer, blocks, mine=(), theirs=()):
    last = bool(mine)
    return pl.pallas_call(
        functools.partial(update_kernel, last),
        in_specs=[pl.BlockSpec(memory_space=pltpu.VMEM)] * (6 + len(mine) + len(theirs)),
        out_specs=[pl.BlockSpec(memory_space=pltpu.VMEM)] * 4,
        out_shape=[PAIR] * 4,
        scratch_shapes=[
            pltpu.VMEM((2, COLS, COLS), F32),
            pltpu.VMEM((2, COLS, COLS), BF16),
            pltpu.VMEM((2, COLS, COLS), BF16),
            pltpu.VMEM((2, 4 * PART, COLS), BF16),
        ],
        compiler_params=params_of(32),
        cost_estimate=cost(2 * 13 * 2 * COLS**3, 8 * MIB),
        name="newton_schulz",
    )(own, peer, *blocks, *mine, *theirs)


def local_kernel(y_ref, p_ref, q_ref, w_ref, out_ref):
    mean = 0.5 * (p_ref[0].astype(F32) + q_ref[0].astype(F32))
    out_ref[0] = (mean - SCALE * w_ref[0].astype(F32)).astype(BF16)


def local(y, d, params, p_peer, w):
    spot = pl.BlockSpec(BLOCK, lambda k, y_ref: natural(2 * d + k, y_ref))
    here = pl.BlockSpec(BLOCK, lambda k, y_ref: (k, 0, 0))
    return pl.pallas_call(
        local_kernel,
        grid_spec=pltpu.PrefetchScalarGridSpec(
            num_scalar_prefetch=1, grid=(2,), in_specs=[spot, spot, here], out_specs=here
        ),
        out_shape=PAIR,
        compiler_params=params_of(8),
        cost_estimate=cost(MIB, 2 * MIB),
        name="local_params",
    )(y, params, p_peer, w)


def mean_kernel(y_ref, a_ref, b_ref, *refs):
    refs[-1][0] = (0.5 * (a_ref[0].astype(F32) + b_ref[0].astype(F32))).astype(BF16)


def mean_into(y, d, own, peer, out):
    here = pl.BlockSpec(BLOCK, lambda k, y_ref: (k, 0, 0))
    held = () if out is None else (out,)
    return pl.pallas_call(
        mean_kernel,
        grid_spec=pltpu.PrefetchScalarGridSpec(
            num_scalar_prefetch=1,
            grid=(2,),
            in_specs=[here, here] + [pl.BlockSpec(memory_space=pl.ANY)] * len(held),
            out_specs=pl.BlockSpec(BLOCK, lambda k, y_ref: natural(2 * d + k, y_ref)),
        ),
        out_shape=WHOLE,
        input_output_aliases={3: 0} if held else {},
        compiler_params=params_of(8),
        cost_estimate=cost(MIB, 2 * MIB),
        name="replica_mean",
    )(y, own, peer, *held)


def flip(value, axis, mask):
    return lax.ppermute(value, axis, [(s, s ^ mask) for s in range(lax.axis_size(axis))])


def shift(value, d):
    count = lax.axis_size("fsdp")
    return lax.ppermute(value, "fsdp", [(s, (s + 2 * d) % count) for s in range(count)])


def gather_rows(groups):
    return [groups[0]] + [shift(groups[d], d) for d in (1, 2, 3)]


def after(value, *earlier):
    return lax.optimization_barrier((value,) + earlier)[0]


def shards(params, momentum, grads):
    y = (lax.axis_index("fsdp") // 2).astype(jnp.int32).reshape(1)
    params, momentum = params[0], momentum[0]

    new0, *nest0 = first_step(y, momentum, grads)
    peer0 = flip(new0, "replica", 1)
    rows0 = gather_rows(nest0)
    second = second_step(y, new0, peer0, grads)
    new1, nest1 = second[:4], second[4:]
    rows1 = gather_rows(nest1)
    p_peer = flip(after(params, peer0), "replica", 1)
    m_peer = [None] * 4
    for d in (0, 1):
        m_peer[d] = flip(new1[d], "replica", 2)

    gram0 = gram(rows0)
    other0 = flip(gram0, "fsdp", 1)
    gram1 = gram(rows1)
    other1 = flip(gram1, "fsdp", 1)

    u_own = update(gram0, other0, rows0)
    u_peer = [flip(u, "replica", 1) for u in u_own]
    for d in (2, 3):
        m_peer[d] = flip(after(new1[d], other1), "replica", 2)

    w = update(gram1, other1, rows1, u_own, u_peer)
    p_own = [None] * 4
    a_peer = [None] * 4
    back = [w[0]] + [shift(w[d], -d) for d in (1, 2, 3)]
    for d in (0, 1, 3, 2):
        p_own[d] = local(y, d, params, p_peer, back[d])
        a_peer[d] = flip(p_own[d], "replica", 2)

    p_out, m_out = None, None
    for d in (0, 1, 2, 3):
        m_out = mean_into(y, d, new1[d], m_peer[d], m_out)
    for d in (0, 1, 3, 2):
        p_out = mean_into(y, d, p_own[d], a_peer[d], p_out)
    return (p_out[None], m_out[None])


def solution(mesh):
    return jax.shard_map(
        shards,
        mesh=mesh,
        in_specs=(
            P("replica", None, "fsdp", None),
            P("replica", None, "fsdp", None),
            P(None, "replica", None, "fsdp", None),
        ),
        out_specs=(P("replica", None, "fsdp", None), P("replica", None, "fsdp", None)),
        check_vma=False,
    )
```

```python
import functools
import math

import jax
import jax.numpy as jnp
from jax import lax
from jax.experimental import pallas as pl
from jax.experimental.pallas import tpu as pltpu
from jax.sharding import PartitionSpec as P

ROWS = 2048
COLS = 512
HALF = COLS // 2
PART = 256
MATS = 8
NS_ITERS = 3
STEPS = 2
PACKED = COLS + 16

BETA = 0.95
LEARN = 0.5
COEF_A = 3.4445
COEF_B = -4.775
COEF_C = 2.0315
SCALE = LEARN * 0.2 * math.sqrt(max(ROWS, COLS))

F32 = jnp.float32
BF16 = jnp.bfloat16
PAIR = jax.ShapeDtypeStruct((2, PART, COLS), BF16)
FOUR = jax.ShapeDtypeStruct((4, PART, COLS), BF16)
WHOLE = jax.ShapeDtypeStruct((MATS, PART, COLS), BF16)
BLOCK = (1, PART, COLS)
MIB = 1 << 20


def mat_of(step, y_ref):
    return (step % 2) * 4 + (y_ref[0] + step // 2) % 4


def natural(step, y_ref):
    return (mat_of(step, y_ref), 0, 0)


def group_spec(place):
    return run_of(2 * place, 2)


def run_of(first, count):
    return pl.BlockSpec(BLOCK, lambda t, y_ref: (jnp.clip(t - first, 0, count - 1), 0, 0))


def params_of(mib):
    return pltpu.CompilerParams(vmem_limit_bytes=mib * MIB)


def cost(flops, nbytes):
    return pl.CostEstimate(flops=flops, bytes_accessed=nbytes, transcendentals=0)


def first_kernel(y_ref, m_ref, g_ref, new_ref, *nest_refs):
    t = pl.program_id(0)
    grad = g_ref[0, 0, 0].astype(F32)
    m_new = (BETA * m_ref[0].astype(F32) + grad).astype(BF16)
    new_ref[0] = m_new
    nest = (grad + BETA * m_new.astype(F32)).astype(BF16)
    for d in range(4):
        @pl.when(t // 2 == d)
        def _():
            nest_refs[d][0] = nest


def first_step(y, momentum, grads):
    return pl.pallas_call(
        first_kernel,
        grid_spec=pltpu.PrefetchScalarGridSpec(
            num_scalar_prefetch=1,
            grid=(MATS,),
            in_specs=[
                pl.BlockSpec(BLOCK, natural),
                pl.BlockSpec((1, 1, 1, PART, COLS), lambda t, y_ref: (0, 0, mat_of(t, y_ref), 0, 0)),
            ],
            out_specs=[pl.BlockSpec(BLOCK, natural)] + [group_spec(d) for d in range(4)],
        ),
        out_shape=[WHOLE] + [PAIR] * 4,
        compiler_params=params_of(16),
        cost_estimate=cost(10 * MIB, 8 * MIB),
        name="nest_first",
    )(y, momentum, grads)


def second_kernel(y_ref, m_ref, peer_ref, g_ref, *out_refs):
    t = pl.program_id(0)
    grad = g_ref[0, 0, 0].astype(F32)
    mean = (0.5 * (m_ref[0].astype(F32) + peer_ref[0].astype(F32))).astype(BF16)
    m_new = (BETA * mean.astype(F32) + grad).astype(BF16)
    nest = (grad + BETA * m_new.astype(F32)).astype(BF16)
    for d in range(4):
        @pl.when(t // 2 == d)
        def _():
            out_refs[max(d - 1, 0)][0] = m_new
            out_refs[3 + d][0] = nest


def second_step(y, m_new, m_peer, grads):
    return pl.pallas_call(
        second_kernel,
        grid_spec=pltpu.PrefetchScalarGridSpec(
            num_scalar_prefetch=1,
            grid=(MATS,),
            in_specs=[
                pl.BlockSpec(BLOCK, natural),
                pl.BlockSpec(BLOCK, natural),
                pl.BlockSpec((1, 1, 1, PART, COLS), lambda t, y_ref: (1, 0, mat_of(t, y_ref), 0, 0)),
            ],
            out_specs=[run_of(0, 4)] + [group_spec(d) for d in (2, 3, 0, 1, 2, 3)],
        ),
        out_shape=[FOUR] + [PAIR] * 6,
        compiler_params=params_of(16),
        cost_estimate=cost(10 * MIB, 10 * MIB),
        name="nest_second",
    )(y, m_new, m_peer, grads)


def iota(axis, shape=(HALF, HALF)):
    return lax.broadcasted_iota(jnp.int32, shape, axis)


def gram_kernel(*refs):
    blocks, out_ref = refs[:4], refs[4]
    left = [ref[0, :, :HALF] for ref in blocks]
    right = [ref[0, :, HALF:] for ref in blocks]

    def product(lhs, rhs):
        total = None
        for one, two in zip(lhs, rhs):
            term = lax.dot_general(one, two, (((0,), (0,)), ((), ())), preferred_element_type=F32)
            total = term if total is None else total + term
        return total

    out_ref[0, :HALF] = product(left, right).astype(BF16)
    top = product(left, left)
    low = product(right, right)
    out_ref[0, HALF:COLS] = jnp.where(iota(1) >= iota(0), top, low).astype(BF16)
    diagonal = jnp.sum(jnp.where(iota(1) == iota(0), low, 0.0), axis=0, keepdims=True)
    out_ref[0, COLS:] = jnp.broadcast_to(diagonal, (PACKED - COLS, HALF)).astype(BF16)


def gram(blocks):
    return pl.pallas_call(
        gram_kernel,
        grid=(2,),
        in_specs=[pl.BlockSpec(BLOCK, lambda k: (k, 0, 0))] * 4,
        out_specs=pl.BlockSpec((1, PACKED, HALF), lambda k: (k, 0, 0)),
        out_shape=jax.ShapeDtypeStruct((2, PACKED, HALF), BF16),
        compiler_params=params_of(16),
        cost_estimate=cost(2 * 2 * 4 * PART * COLS * COLS, 3 * MIB),
        name="partial_gram",
    )(*blocks)


def dot(lhs, rhs):
    return jnp.dot(lhs, rhs, preferred_element_type=F32)


def update_kernel(last, *refs):
    own_ref, peer_ref = refs[:2]
    x_refs = refs[2:6]
    if last:
        u_refs, v_refs = refs[6:10], refs[10:14]
        out_refs = refs[14:18]
        rest = refs[18:]
    else:
        out_refs = refs[6:10]
        rest = refs[10:]
    g_ref, gb_ref, r_ref, y_ref = rest
    inverse = []
    for k in range(2):
        packed = own_ref[k].astype(F32) + peer_ref[k].astype(F32)
        cross = packed[:HALF]
        mixed = packed[HALF:COLS]
        flipped = mixed.T
        top = jnp.where(iota(1) >= iota(0), mixed, flipped)
        low = jnp.where(iota(1) < iota(0), mixed, flipped)
        low = jnp.where(iota(1) == iota(0), packed[COLS : COLS + 1], low)
        diagonal = jnp.sum(jnp.where(iota(1) == iota(0), top, 0.0), axis=0, keepdims=True)
        diagonal += packed[COLS : COLS + 1]
        trace = jnp.sum(diagonal, axis=1, keepdims=True)
        inv = 1.0 / (jnp.sqrt(trace) + 1e-07)
        inverse.append(inv)
        g_ref[k, :HALF, :HALF] = top * inv * inv
        g_ref[k, :HALF, HALF:] = cross * inv * inv
        g_ref[k, HALF:, :HALF] = cross.T * inv * inv
        g_ref[k, HALF:, HALF:] = low * inv * inv
        gb_ref[k] = g_ref[k].astype(BF16)
    for d in range(4):
        for k in range(2):
            y_ref[k, d * PART : (d + 1) * PART] = (x_refs[d][k].astype(F32) * inverse[k]).astype(BF16)
    for step in range(NS_ITERS):
        for k in range(2):
            value = COEF_B * g_ref[k] + COEF_C * dot(gb_ref[k], gb_ref[k])
            r_ref[k] = value.astype(BF16)
        if step < NS_ITERS - 1:
            for k in range(2):
                value = COEF_A * g_ref[k] + dot(gb_ref[k], r_ref[k])
                g_ref[k] = value
                gb_ref[k] = value.astype(BF16)
            for k in range(2):
                value = COEF_A * g_ref[k] + dot(gb_ref[k], r_ref[k])
                g_ref[k] = value
                gb_ref[k] = value.astype(BF16)
        for d in range(4):
            for k in range(2):
                block = y_ref[k, d * PART : (d + 1) * PART]
                value = COEF_A * block.astype(F32) + dot(block, r_ref[k])
                if step < NS_ITERS - 1:
                    y_ref[k, d * PART : (d + 1) * PART] = value.astype(BF16)
                elif last:
                    mean = 0.5 * (u_refs[d][k].astype(F32) + v_refs[d][k].astype(F32))
                    out_refs[d][k] = (value + mean).astype(BF16)
                else:
                    out_refs[d][k] = value.astype(BF16)


def update(own, peer, blocks, mine=(), theirs=()):
    last = bool(mine)
    return pl.pallas_call(
        functools.partial(update_kernel, last),
        in_specs=[pl.BlockSpec(memory_space=pltpu.VMEM)] * (6 + len(mine) + len(theirs)),
        out_specs=[pl.BlockSpec(memory_space=pltpu.VMEM)] * 4,
        out_shape=[PAIR] * 4,
        scratch_shapes=[
            pltpu.VMEM((2, COLS, COLS), F32),
            pltpu.VMEM((2, COLS, COLS), BF16),
            pltpu.VMEM((2, COLS, COLS), BF16),
            pltpu.VMEM((2, 4 * PART, COLS), BF16),
        ],
        compiler_params=params_of(32),
        cost_estimate=cost(2 * 13 * 2 * COLS**3, 8 * MIB),
        name="newton_schulz",
    )(own, peer, *blocks, *mine, *theirs)


def local_kernel(y_ref, p_ref, q_ref, w_ref, out_ref):
    mean = 0.5 * (p_ref[0].astype(F32) + q_ref[0].astype(F32))
    out_ref[0] = (mean - SCALE * w_ref[0].astype(F32)).astype(BF16)


def local(y, d, params, p_peer, w):
    spot = pl.BlockSpec(BLOCK, lambda k, y_ref: natural(2 * d + k, y_ref))
    here = pl.BlockSpec(BLOCK, lambda k, y_ref: (k, 0, 0))
    return pl.pallas_call(
        local_kernel,
        grid_spec=pltpu.PrefetchScalarGridSpec(
            num_scalar_prefetch=1, grid=(2,), in_specs=[spot, spot, here], out_specs=here
        ),
        out_shape=PAIR,
        compiler_params=params_of(8),
        cost_estimate=cost(MIB, 2 * MIB),
        name="local_params",
    )(y, params, p_peer, w)


def mean_kernel(y_ref, a_ref, b_ref, *refs):
    refs[-1][0] = (0.5 * (a_ref[0].astype(F32) + b_ref[0].astype(F32))).astype(BF16)


def mean_into(y, d, own, peer, out):
    count = own.shape[0]
    here = run_of(0, count)
    held = () if out is None else (out,)
    return pl.pallas_call(
        mean_kernel,
        grid_spec=pltpu.PrefetchScalarGridSpec(
            num_scalar_prefetch=1,
            grid=(count,),
            in_specs=[here, here] + [pl.BlockSpec(memory_space=pl.ANY)] * len(held),
            out_specs=pl.BlockSpec(BLOCK, lambda t, y_ref: natural(2 * d + t, y_ref)),
        ),
        out_shape=WHOLE,
        input_output_aliases={3: 0} if held else {},
        compiler_params=params_of(8),
        cost_estimate=cost(MIB, 2 * MIB),
        name="replica_mean",
    )(y, own, peer, *held)


def flip(value, axis, mask):
    return lax.ppermute(value, axis, [(s, s ^ mask) for s in range(lax.axis_size(axis))])


def shift(value, d):
    count = lax.axis_size("fsdp")
    return lax.ppermute(value, "fsdp", [(s, (s + 2 * d) % count) for s in range(count)])


def gather_rows(groups):
    return [groups[0]] + [shift(groups[d], d) for d in (1, 2, 3)]


def after(values, *earlier):
    return lax.optimization_barrier((values,) + earlier)[0]


def shards(params, momentum, grads):
    y = (lax.axis_index("fsdp") // 2).astype(jnp.int32).reshape(1)
    params, momentum = params[0], momentum[0]

    new0, *nest0 = first_step(y, momentum, grads)
    peer0 = flip(new0, "replica", 1)
    p_peer = flip(after(params, peer0), "replica", 1)
    rows0 = gather_rows(nest0)
    ma, mb, mc, *nest1 = second_step(y, new0, peer0, grads)
    ma_peer = flip(ma, "replica", 2)

    rows0 = after(rows0, ma, p_peer)
    gram0 = gram(rows0)
    other0 = flip(gram0, "fsdp", 1)
    rows1 = gather_rows(after(nest1, gram0))
    gram1 = gram(after(rows1, ma_peer))
    other1 = flip(gram1, "fsdp", 1)
    mb_peer = flip(after(mb, gram0), "replica", 2)

    u_own = update(gram0, after(other0, gram1), rows0)
    u_peer = [flip(u, "replica", 1) for u in u_own]

    mc_peer = flip(after(mc, other1), "replica", 2)
    w = update(gram1, after(other1, mb_peer), rows1, u_own, u_peer)
    back = [w[0]] + [shift(w[d], -d) for d in (1, 2, 3)]
    p_own = [None] * 4
    a_peer = [None] * 4
    p_own[0] = local(y, 0, params, p_peer, back[0])
    a_peer[0] = flip(p_own[0], "replica", 2)
    p_own[1] = local(y, 1, params, p_peer, after(back[1], p_own[0]))
    a_peer[1] = flip(p_own[1], "replica", 2)
    p_own[3] = local(y, 3, params, p_peer, after(back[3], p_own[1]))
    a_peer[3] = flip(p_own[3], "replica", 2)
    p_own[2] = local(y, 2, params, p_peer, after(back[2], p_own[3], a_peer[0], mc_peer))
    a_peer[2] = flip(p_own[2], "replica", 2)

    m_out = mean_into(y, 0, ma, ma_peer, None)
    m_out = mean_into(y, 2, mb, mb_peer, m_out)
    m_out = mean_into(y, 3, mc, mc_peer, m_out)
    p_out = None
    for d in (0, 1, 3, 2):
        p_out = mean_into(y, d, p_own[d], after(a_peer[d], m_out), p_out)
    return (p_out[None], m_out[None])


def solution(mesh):
    return jax.shard_map(
        shards,
        mesh=mesh,
        in_specs=(
            P("replica", None, "fsdp", None),
            P("replica", None, "fsdp", None),
            P(None, "replica", None, "fsdp", None),
        ),
        out_specs=(P("replica", None, "fsdp", None), P("replica", None, "fsdp", None)),
        check_vma=False,
    )
```

```python
import functools
import math

import jax
import jax.numpy as jnp
from jax import lax
from jax.experimental import pallas as pl
from jax.experimental.pallas import tpu as pltpu
from jax.sharding import PartitionSpec as P

ROWS = 2048
COLS = 512
HALF = COLS // 2
PART = 256
MATS = 8
NS_ITERS = 3
STEPS = 2
PACKED = COLS + 16

BETA = 0.95
LEARN = 0.5
COEF_A = 3.4445
COEF_B = -4.775
COEF_C = 2.0315
SCALE = LEARN * 0.2 * math.sqrt(max(ROWS, COLS))

F32 = jnp.float32
BF16 = jnp.bfloat16
PAIR = jax.ShapeDtypeStruct((2, PART, COLS), BF16)
SIX = jax.ShapeDtypeStruct((6, PART, COLS), BF16)
WHOLE = jax.ShapeDtypeStruct((MATS, PART, COLS), BF16)
BLOCK = (1, PART, COLS)
MIB = 1 << 20


def mat_of(step, y_ref):
    return (step % 2) * 4 + (y_ref[0] + step // 2) % 4


def natural(step, y_ref):
    return (mat_of(step, y_ref), 0, 0)


def group_spec(place):
    return run_of(2 * place, 2)


def run_of(first, count):
    return pl.BlockSpec(BLOCK, lambda t, y_ref: (jnp.clip(t - first, 0, count - 1), 0, 0))


def params_of(mib):
    return pltpu.CompilerParams(vmem_limit_bytes=mib * MIB)


def cost(flops, nbytes):
    return pl.CostEstimate(flops=flops, bytes_accessed=nbytes, transcendentals=0)


def first_kernel(y_ref, m_ref, g_ref, new_ref, *nest_refs):
    t = pl.program_id(0)
    grad = g_ref[0, 0, 0].astype(F32)
    m_new = (BETA * m_ref[0].astype(F32) + grad).astype(BF16)
    new_ref[0] = m_new
    nest = (grad + BETA * m_new.astype(F32)).astype(BF16)
    for d in range(4):
        @pl.when(t // 2 == d)
        def _():
            nest_refs[d][0] = nest


def first_step(y, momentum, grads):
    return pl.pallas_call(
        first_kernel,
        grid_spec=pltpu.PrefetchScalarGridSpec(
            num_scalar_prefetch=1,
            grid=(MATS,),
            in_specs=[
                pl.BlockSpec(BLOCK, natural),
                pl.BlockSpec((1, 1, 1, PART, COLS), lambda t, y_ref: (0, 0, mat_of(t, y_ref), 0, 0)),
            ],
            out_specs=[pl.BlockSpec(BLOCK, natural)] + [group_spec(d) for d in range(4)],
        ),
        out_shape=[WHOLE] + [PAIR] * 4,
        compiler_params=params_of(16),
        cost_estimate=cost(10 * MIB, 8 * MIB),
        name="nest_first",
    )(y, momentum, grads)


def second_kernel(y_ref, m_ref, peer_ref, g_ref, *out_refs):
    t = pl.program_id(0)
    grad = g_ref[0, 0, 0].astype(F32)
    mean = (0.5 * (m_ref[0].astype(F32) + peer_ref[0].astype(F32))).astype(BF16)
    m_new = (BETA * mean.astype(F32) + grad).astype(BF16)
    nest = (grad + BETA * m_new.astype(F32)).astype(BF16)
    for d in range(4):
        @pl.when(t // 2 == d)
        def _():
            out_refs[d // 3][0] = m_new
            out_refs[2 + d][0] = nest


def second_step(y, m_new, m_peer, grads):
    return pl.pallas_call(
        second_kernel,
        grid_spec=pltpu.PrefetchScalarGridSpec(
            num_scalar_prefetch=1,
            grid=(MATS,),
            in_specs=[
                pl.BlockSpec(BLOCK, natural),
                pl.BlockSpec(BLOCK, natural),
                pl.BlockSpec((1, 1, 1, PART, COLS), lambda t, y_ref: (1, 0, mat_of(t, y_ref), 0, 0)),
            ],
            out_specs=[run_of(0, 6), run_of(6, 2)] + [group_spec(d) for d in range(4)],
        ),
        out_shape=[SIX] + [PAIR] * 5,
        compiler_params=params_of(16),
        cost_estimate=cost(10 * MIB, 10 * MIB),
        name="nest_second",
    )(y, m_new, m_peer, grads)


def iota(axis, shape=(HALF, HALF)):
    return lax.broadcasted_iota(jnp.int32, shape, axis)


def gram_kernel(*refs):
    blocks, out_ref = refs[:4], refs[4]
    left = [ref[0, :, :HALF] for ref in blocks]
    right = [ref[0, :, HALF:] for ref in blocks]

    def product(lhs, rhs):
        total = None
        for one, two in zip(lhs, rhs):
            term = lax.dot_general(one, two, (((0,), (0,)), ((), ())), preferred_element_type=F32)
            total = term if total is None else total + term
        return total

    out_ref[0, :HALF] = product(left, right).astype(BF16)
    top = product(left, left)
    low = product(right, right)
    out_ref[0, HALF:COLS] = jnp.where(iota(1) >= iota(0), top, low).astype(BF16)
    diagonal = jnp.sum(jnp.where(iota(1) == iota(0), low, 0.0), axis=0, keepdims=True)
    out_ref[0, COLS:] = jnp.broadcast_to(diagonal, (PACKED - COLS, HALF)).astype(BF16)


def gram(blocks):
    return pl.pallas_call(
        gram_kernel,
        grid=(2,),
        in_specs=[pl.BlockSpec(BLOCK, lambda k: (k, 0, 0))] * 4,
        out_specs=pl.BlockSpec((1, PACKED, HALF), lambda k: (k, 0, 0)),
        out_shape=jax.ShapeDtypeStruct((2, PACKED, HALF), BF16),
        compiler_params=params_of(16),
        cost_estimate=cost(2 * 2 * 4 * PART * COLS * COLS, 3 * MIB),
        name="partial_gram",
    )(*blocks)


def dot(lhs, rhs):
    return jnp.dot(lhs, rhs, preferred_element_type=F32)


def update_kernel(last, *refs):
    own_ref, peer_ref = refs[:2]
    x_refs = refs[2:6]
    if last:
        u_refs, v_refs = refs[6:10], refs[10:14]
        out_refs = refs[14:18]
        rest = refs[18:]
    else:
        out_refs = refs[6:10]
        rest = refs[10:]
    g_ref, gb_ref, r_ref, y_ref = rest
    inverse = []
    for k in range(2):
        packed = own_ref[k].astype(F32) + peer_ref[k].astype(F32)
        cross = packed[:HALF]
        mixed = packed[HALF:COLS]
        flipped = mixed.T
        top = jnp.where(iota(1) >= iota(0), mixed, flipped)
        low = jnp.where(iota(1) < iota(0), mixed, flipped)
        low = jnp.where(iota(1) == iota(0), packed[COLS : COLS + 1], low)
        diagonal = jnp.sum(jnp.where(iota(1) == iota(0), top, 0.0), axis=0, keepdims=True)
        diagonal += packed[COLS : COLS + 1]
        trace = jnp.sum(diagonal, axis=1, keepdims=True)
        inv = 1.0 / (jnp.sqrt(trace) + 1e-07)
        inverse.append(inv)
        g_ref[k, :HALF, :HALF] = top * inv * inv
        g_ref[k, :HALF, HALF:] = cross * inv * inv
        g_ref[k, HALF:, :HALF] = cross.T * inv * inv
        g_ref[k, HALF:, HALF:] = low * inv * inv
        gb_ref[k] = g_ref[k].astype(BF16)
    for d in range(4):
        for k in range(2):
            y_ref[k, d * PART : (d + 1) * PART] = (x_refs[d][k].astype(F32) * inverse[k]).astype(BF16)
    for step in range(NS_ITERS):
        for k in range(2):
            value = COEF_B * g_ref[k] + COEF_C * dot(gb_ref[k], gb_ref[k])
            r_ref[k] = value.astype(BF16)
        if step < NS_ITERS - 1:
            for k in range(2):
                value = COEF_A * g_ref[k] + dot(gb_ref[k], r_ref[k])
                g_ref[k] = value
                gb_ref[k] = value.astype(BF16)
            for k in range(2):
                value = COEF_A * g_ref[k] + dot(gb_ref[k], r_ref[k])
                g_ref[k] = value
                gb_ref[k] = value.astype(BF16)
        for d in range(4):
            for k in range(2):
                block = y_ref[k, d * PART : (d + 1) * PART]
                value = COEF_A * block.astype(F32) + dot(block, r_ref[k])
                if step < NS_ITERS - 1:
                    y_ref[k, d * PART : (d + 1) * PART] = value.astype(BF16)
                elif last:
                    mean = 0.5 * (u_refs[d][k].astype(F32) + v_refs[d][k].astype(F32))
                    out_refs[d][k] = (value + mean).astype(BF16)
                else:
                    out_refs[d][k] = value.astype(BF16)


def update(own, peer, blocks, mine=(), theirs=()):
    last = bool(mine)
    return pl.pallas_call(
        functools.partial(update_kernel, last),
        in_specs=[pl.BlockSpec(memory_space=pltpu.VMEM)] * (6 + len(mine) + len(theirs)),
        out_specs=[pl.BlockSpec(memory_space=pltpu.VMEM)] * 4,
        out_shape=[PAIR] * 4,
        scratch_shapes=[
            pltpu.VMEM((2, COLS, COLS), F32),
            pltpu.VMEM((2, COLS, COLS), BF16),
            pltpu.VMEM((2, COLS, COLS), BF16),
            pltpu.VMEM((2, 4 * PART, COLS), BF16),
        ],
        compiler_params=params_of(32),
        cost_estimate=cost(2 * 13 * 2 * COLS**3, 8 * MIB),
        name="newton_schulz",
    )(own, peer, *blocks, *mine, *theirs)


def local_kernel(y_ref, p_ref, q_ref, w_ref, out_ref):
    mean = 0.5 * (p_ref[0].astype(F32) + q_ref[0].astype(F32))
    out_ref[0] = (mean - SCALE * w_ref[0].astype(F32)).astype(BF16)


def local(y, d, params, p_peer, w):
    spot = pl.BlockSpec(BLOCK, lambda k, y_ref: natural(2 * d + k, y_ref))
    here = pl.BlockSpec(BLOCK, lambda k, y_ref: (k, 0, 0))
    return pl.pallas_call(
        local_kernel,
        grid_spec=pltpu.PrefetchScalarGridSpec(
            num_scalar_prefetch=1, grid=(2,), in_specs=[spot, spot, here], out_specs=here
        ),
        out_shape=PAIR,
        compiler_params=params_of(8),
        cost_estimate=cost(MIB, 2 * MIB),
        name="local_params",
    )(y, params, p_peer, w)


def mean_kernel(y_ref, a_ref, b_ref, *refs):
    refs[-1][0] = (0.5 * (a_ref[0].astype(F32) + b_ref[0].astype(F32))).astype(BF16)


def mean_into(y, d, own, peer, out):
    count = own.shape[0]
    here = run_of(0, count)
    held = () if out is None else (out,)
    return pl.pallas_call(
        mean_kernel,
        grid_spec=pltpu.PrefetchScalarGridSpec(
            num_scalar_prefetch=1,
            grid=(count,),
            in_specs=[here, here] + [pl.BlockSpec(memory_space=pl.ANY)] * len(held),
            out_specs=pl.BlockSpec(BLOCK, lambda t, y_ref: natural(2 * d + t, y_ref)),
        ),
        out_shape=WHOLE,
        input_output_aliases={3: 0} if held else {},
        compiler_params=params_of(8),
        cost_estimate=cost(MIB, 2 * MIB),
        name="replica_mean",
    )(y, own, peer, *held)


def flip(value, axis, mask):
    return lax.ppermute(value, axis, [(s, s ^ mask) for s in range(lax.axis_size(axis))])


def shift(value, d):
    count = lax.axis_size("fsdp")
    return lax.ppermute(value, "fsdp", [(s, (s + 2 * d) % count) for s in range(count)])


def gather_rows(groups):
    return [groups[0]] + [shift(groups[d], d) for d in (1, 2, 3)]


def after(values, *earlier):
    return lax.optimization_barrier((values,) + earlier)[0]


def shards(params, momentum, grads):
    y = (lax.axis_index("fsdp") // 2).astype(jnp.int32).reshape(1)
    params, momentum = params[0], momentum[0]

    new0, *nest0 = first_step(y, momentum, grads)
    peer0 = flip(new0, "replica", 1)
    p_peer = flip(after(params, peer0), "replica", 1)
    rows0 = gather_rows(nest0)
    ma, mb, *nest1 = second_step(y, new0, peer0, grads)
    ma_peer = flip(ma, "replica", 2)

    rows0 = after(rows0, ma, p_peer)
    gram0 = gram(rows0)
    other0 = flip(gram0, "fsdp", 1)
    rows1 = gather_rows(after(nest1, gram0))
    gram1 = gram(rows1)
    other1 = flip(gram1, "fsdp", 1)
    mb_peer = flip(after(mb, gram0), "replica", 2)

    u_own = update(gram0, after(other0, gram1), rows0)
    u_peer = [flip(u, "replica", 1) for u in u_own]

    w = update(gram1, after(other1, mb_peer, ma_peer), rows1, u_own, u_peer)
    back = [w[0], shift(w[1], -1), None, shift(w[3], -3)]
    back[2] = shift(after(w[2], back[1]), -2)
    p_own = [None] * 4
    a_peer = [None] * 4
    p_own[0] = local(y, 0, params, p_peer, back[0])
    a_peer[0] = flip(p_own[0], "replica", 2)
    p_own[1] = local(y, 1, params, p_peer, after(back[1], p_own[0]))
    a_peer[1] = flip(p_own[1], "replica", 2)
    p_own[3] = local(y, 3, params, p_peer, after(back[3], p_own[1]))
    a_peer[3] = flip(p_own[3], "replica", 2)
    p_own[2] = local(y, 2, params, p_peer, after(back[2], p_own[3], a_peer[0], a_peer[1]))
    a_peer[2] = flip(p_own[2], "replica", 2)

    m_out = mean_into(y, 0, ma, ma_peer, None)
    m_out = mean_into(y, 3, mb, mb_peer, m_out)
    p_out = None
    for d in (0, 1, 3, 2):
        p_out = mean_into(y, d, p_own[d], after(a_peer[d], m_out), p_out)
    return (p_out[None], m_out[None])


def solution(mesh):
    return jax.shard_map(
        shards,
        mesh=mesh,
        in_specs=(
            P("replica", None, "fsdp", None),
            P("replica", None, "fsdp", None),
            P(None, "replica", None, "fsdp", None),
        ),
        out_specs=(P("replica", None, "fsdp", None), P("replica", None, "fsdp", None)),
        check_vma=False,
    )
```

```python
import functools
import math

import jax
import jax.numpy as jnp
from jax import lax
from jax.experimental import pallas as pl
from jax.experimental.pallas import tpu as pltpu
from jax.sharding import PartitionSpec as P

ROWS = 2048
COLS = 512
HALF = COLS // 2
PART = 256
MATS = 8
NS_ITERS = 3
STEPS = 2
PACKED = COLS + 16

BETA = 0.95
LEARN = 0.5
COEF_A = 3.4445
COEF_B = -4.775
COEF_C = 2.0315
SCALE = LEARN * 0.2 * math.sqrt(max(ROWS, COLS))

F32 = jnp.float32
BF16 = jnp.bfloat16
PAIR = jax.ShapeDtypeStruct((2, PART, COLS), BF16)
SIX = jax.ShapeDtypeStruct((6, PART, COLS), BF16)
WHOLE = jax.ShapeDtypeStruct((MATS, PART, COLS), BF16)
BLOCK = (1, PART, COLS)
MIB = 1 << 20


def mat_of(step, y_ref):
    return (step % 2) * 4 + (y_ref[0] + step // 2) % 4


def natural(step, y_ref):
    return (mat_of(step, y_ref), 0, 0)


def group_spec(place):
    return run_of(2 * place, 2)


def run_of(first, count):
    return pl.BlockSpec(BLOCK, lambda t, y_ref: (jnp.clip(t - first, 0, count - 1), 0, 0))


def params_of(mib):
    return pltpu.CompilerParams(vmem_limit_bytes=mib * MIB)


def cost(flops, nbytes):
    return pl.CostEstimate(flops=flops, bytes_accessed=nbytes, transcendentals=0)


def first_kernel(y_ref, m_ref, g_ref, new_ref, *nest_refs):
    t = pl.program_id(0)
    grad = g_ref[0, 0, 0].astype(F32)
    m_new = (BETA * m_ref[0].astype(F32) + grad).astype(BF16)
    new_ref[0] = m_new
    nest = (grad + BETA * m_new.astype(F32)).astype(BF16)
    for d in range(4):
        @pl.when(t // 2 == d)
        def _():
            nest_refs[d][0] = nest


def first_step(y, momentum, grads):
    return pl.pallas_call(
        first_kernel,
        grid_spec=pltpu.PrefetchScalarGridSpec(
            num_scalar_prefetch=1,
            grid=(MATS,),
            in_specs=[
                pl.BlockSpec(BLOCK, natural),
                pl.BlockSpec((1, 1, 1, PART, COLS), lambda t, y_ref: (0, 0, mat_of(t, y_ref), 0, 0)),
            ],
            out_specs=[pl.BlockSpec(BLOCK, natural)] + [group_spec(d) for d in range(4)],
        ),
        out_shape=[WHOLE] + [PAIR] * 4,
        compiler_params=params_of(16),
        cost_estimate=cost(10 * MIB, 8 * MIB),
        name="nest_first",
    )(y, momentum, grads)


def second_kernel(y_ref, m_ref, peer_ref, g_ref, *out_refs):
    t = pl.program_id(0)
    grad = g_ref[0, 0, 0].astype(F32)
    mean = (0.5 * (m_ref[0].astype(F32) + peer_ref[0].astype(F32))).astype(BF16)
    m_new = (BETA * mean.astype(F32) + grad).astype(BF16)
    nest = (grad + BETA * m_new.astype(F32)).astype(BF16)
    for d in range(4):
        @pl.when(t // 2 == d)
        def _():
            out_refs[d // 3][0] = m_new
            out_refs[2 + d][0] = nest


def second_step(y, m_new, m_peer, grads):
    return pl.pallas_call(
        second_kernel,
        grid_spec=pltpu.PrefetchScalarGridSpec(
            num_scalar_prefetch=1,
            grid=(MATS,),
            in_specs=[
                pl.BlockSpec(BLOCK, natural),
                pl.BlockSpec(BLOCK, natural),
                pl.BlockSpec((1, 1, 1, PART, COLS), lambda t, y_ref: (1, 0, mat_of(t, y_ref), 0, 0)),
            ],
            out_specs=[run_of(0, 6), run_of(6, 2)] + [group_spec(d) for d in range(4)],
        ),
        out_shape=[SIX] + [PAIR] * 5,
        compiler_params=params_of(16),
        cost_estimate=cost(10 * MIB, 10 * MIB),
        name="nest_second",
    )(y, m_new, m_peer, grads)


def iota(axis, shape=(HALF, HALF)):
    return lax.broadcasted_iota(jnp.int32, shape, axis)


def gram_kernel(*refs):
    blocks, out_ref = refs[:4], refs[4]
    left = [ref[0, :, :HALF] for ref in blocks]
    right = [ref[0, :, HALF:] for ref in blocks]

    def product(lhs, rhs):
        total = None
        for one, two in zip(lhs, rhs):
            term = lax.dot_general(one, two, (((0,), (0,)), ((), ())), preferred_element_type=F32)
            total = term if total is None else total + term
        return total

    out_ref[0, :HALF] = product(left, right).astype(BF16)
    top = product(left, left)
    low = product(right, right)
    out_ref[0, HALF:COLS] = jnp.where(iota(1) >= iota(0), top, low).astype(BF16)
    diagonal = jnp.sum(jnp.where(iota(1) == iota(0), low, 0.0), axis=0, keepdims=True)
    out_ref[0, COLS:] = jnp.broadcast_to(diagonal, (PACKED - COLS, HALF)).astype(BF16)


def gram(blocks):
    return pl.pallas_call(
        gram_kernel,
        grid=(2,),
        in_specs=[pl.BlockSpec(BLOCK, lambda k: (k, 0, 0))] * 4,
        out_specs=pl.BlockSpec((1, PACKED, HALF), lambda k: (k, 0, 0)),
        out_shape=jax.ShapeDtypeStruct((2, PACKED, HALF), BF16),
        compiler_params=params_of(16),
        cost_estimate=cost(2 * 2 * 4 * PART * COLS * COLS, 3 * MIB),
        name="partial_gram",
    )(*blocks)


def dot(lhs, rhs):
    return jnp.dot(lhs, rhs, preferred_element_type=F32)


def update_kernel(last, *refs):
    own_ref, peer_ref = refs[:2]
    x_refs = refs[2:6]
    if last:
        u_refs, v_refs = refs[6:10], refs[10:14]
        out_refs = refs[14:18]
        rest = refs[18:]
    else:
        out_refs = refs[6:10]
        rest = refs[10:]
    g_ref, gb_ref, r_ref, y_ref = rest
    inverse = []
    for k in range(2):
        packed = own_ref[k].astype(F32) + peer_ref[k].astype(F32)
        cross = packed[:HALF]
        mixed = packed[HALF:COLS]
        flipped = mixed.T
        top = jnp.where(iota(1) >= iota(0), mixed, flipped)
        low = jnp.where(iota(1) < iota(0), mixed, flipped)
        low = jnp.where(iota(1) == iota(0), packed[COLS : COLS + 1], low)
        diagonal = jnp.sum(jnp.where(iota(1) == iota(0), top, 0.0), axis=0, keepdims=True)
        diagonal += packed[COLS : COLS + 1]
        trace = jnp.sum(diagonal, axis=1, keepdims=True)
        inv = 1.0 / (jnp.sqrt(trace) + 1e-07)
        inverse.append(inv)
        g_ref[k, :HALF, :HALF] = top * inv * inv
        g_ref[k, :HALF, HALF:] = cross * inv * inv
        g_ref[k, HALF:, :HALF] = cross.T * inv * inv
        g_ref[k, HALF:, HALF:] = low * inv * inv
        gb_ref[k] = g_ref[k].astype(BF16)
    for d in range(4):
        for k in range(2):
            y_ref[k, d * PART : (d + 1) * PART] = (x_refs[d][k].astype(F32) * inverse[k]).astype(BF16)
    for step in range(NS_ITERS):
        for k in range(2):
            value = COEF_B * g_ref[k] + COEF_C * dot(gb_ref[k], gb_ref[k])
            r_ref[k] = value.astype(BF16)
        if step < NS_ITERS - 1:
            for k in range(2):
                value = COEF_A * g_ref[k] + dot(gb_ref[k], r_ref[k])
                g_ref[k] = value
                gb_ref[k] = value.astype(BF16)
            for k in range(2):
                value = COEF_A * g_ref[k] + dot(gb_ref[k], r_ref[k])
                g_ref[k] = value
                gb_ref[k] = value.astype(BF16)
        for d in range(4):
            for k in range(2):
                block = y_ref[k, d * PART : (d + 1) * PART]
                value = COEF_A * block.astype(F32) + dot(block, r_ref[k])
                if step < NS_ITERS - 1:
                    y_ref[k, d * PART : (d + 1) * PART] = value.astype(BF16)
                elif last:
                    mean = 0.5 * (u_refs[d][k].astype(F32) + v_refs[d][k].astype(F32))
                    out_refs[d][k] = (value + mean).astype(BF16)
                else:
                    out_refs[d][k] = value.astype(BF16)


def update(own, peer, blocks, mine=(), theirs=()):
    last = bool(mine)
    return pl.pallas_call(
        functools.partial(update_kernel, last),
        in_specs=[pl.BlockSpec(memory_space=pltpu.VMEM)] * (6 + len(mine) + len(theirs)),
        out_specs=[pl.BlockSpec(memory_space=pltpu.VMEM)] * 4,
        out_shape=[PAIR] * 4,
        scratch_shapes=[
            pltpu.VMEM((2, COLS, COLS), F32),
            pltpu.VMEM((2, COLS, COLS), BF16),
            pltpu.VMEM((2, COLS, COLS), BF16),
            pltpu.VMEM((2, 4 * PART, COLS), BF16),
        ],
        compiler_params=params_of(32),
        cost_estimate=cost(2 * 13 * 2 * COLS**3, 8 * MIB),
        name="newton_schulz",
    )(own, peer, *blocks, *mine, *theirs)


def local_kernel(y_ref, p_ref, q_ref, w_ref, out_ref):
    mean = 0.5 * (p_ref[0].astype(F32) + q_ref[0].astype(F32))
    out_ref[0] = (mean - SCALE * w_ref[0].astype(F32)).astype(BF16)


def local(y, d, params, p_peer, w):
    spot = pl.BlockSpec(BLOCK, lambda k, y_ref: natural(2 * d + k, y_ref))
    here = pl.BlockSpec(BLOCK, lambda k, y_ref: (k, 0, 0))
    return pl.pallas_call(
        local_kernel,
        grid_spec=pltpu.PrefetchScalarGridSpec(
            num_scalar_prefetch=1, grid=(2,), in_specs=[spot, spot, here], out_specs=here
        ),
        out_shape=PAIR,
        compiler_params=params_of(8),
        cost_estimate=cost(MIB, 2 * MIB),
        name="local_params",
    )(y, params, p_peer, w)


def mean_kernel(y_ref, a_ref, b_ref, *refs):
    refs[-1][0] = (0.5 * (a_ref[0].astype(F32) + b_ref[0].astype(F32))).astype(BF16)


def mean_into(y, d, own, peer, out):
    count = own.shape[0]
    here = run_of(0, count)
    held = () if out is None else (out,)
    return pl.pallas_call(
        mean_kernel,
        grid_spec=pltpu.PrefetchScalarGridSpec(
            num_scalar_prefetch=1,
            grid=(count,),
            in_specs=[here, here] + [pl.BlockSpec(memory_space=pl.ANY)] * len(held),
            out_specs=pl.BlockSpec(BLOCK, lambda t, y_ref: natural(2 * d + t, y_ref)),
        ),
        out_shape=WHOLE,
        input_output_aliases={3: 0} if held else {},
        compiler_params=params_of(8),
        cost_estimate=cost(MIB, 2 * MIB),
        name="replica_mean",
    )(y, own, peer, *held)


def flip(value, axis, mask):
    return lax.ppermute(value, axis, [(s, s ^ mask) for s in range(lax.axis_size(axis))])


def shift(value, d):
    count = lax.axis_size("fsdp")
    return lax.ppermute(value, "fsdp", [(s, (s + 2 * d) % count) for s in range(count)])


def gather_rows(groups):
    return [groups[0]] + [shift(groups[d], d) for d in (1, 2, 3)]


def after(values, *earlier):
    return lax.optimization_barrier((values,) + earlier)[0]


def shards(params, momentum, grads):
    y = (lax.axis_index("fsdp") // 2).astype(jnp.int32).reshape(1)
    params, momentum = params[0], momentum[0]

    new0, *nest0 = first_step(y, momentum, grads)
    peer0 = flip(new0, "replica", 1)
    p_peer = flip(after(params, peer0), "replica", 1)
    rows0 = gather_rows(nest0)
    ma, mb, *nest1 = second_step(y, new0, peer0, grads)
    ma_peer = flip(ma, "replica", 2)

    rows0 = after(rows0, ma, p_peer)
    gram0 = gram(rows0)
    other0 = flip(gram0, "fsdp", 1)
    rows1 = gather_rows(after(nest1, gram0))
    gram1 = gram(rows1)
    other1 = flip(gram1, "fsdp", 1)
    mb_peer = flip(after(mb, gram0), "replica", 2)

    u_own = update(gram0, after(other0, gram1), rows0)
    u_peer = [flip(u, "replica", 1) for u in u_own]

    w = update(gram1, after(other1, ma_peer), rows1, u_own, u_peer)
    back = [w[0], shift(w[1], -1), None, shift(w[3], -3)]
    back[2] = shift(after(w[2], back[1]), -2)
    p_own = [None] * 4
    a_peer = [None] * 4
    p_own[0] = local(y, 0, params, p_peer, back[0])
    a_peer[0] = flip(p_own[0], "replica", 2)
    p_own[1] = local(y, 1, params, p_peer, after(back[1], p_own[0], mb_peer))
    a_peer[1] = flip(p_own[1], "replica", 2)
    p_own[3] = local(y, 3, params, p_peer, after(back[3], p_own[1]))
    a_peer[3] = flip(p_own[3], "replica", 2)
    p_own[2] = local(y, 2, params, p_peer, after(back[2], p_own[3], a_peer[0], a_peer[1]))
    a_peer[2] = flip(p_own[2], "replica", 2)

    m_out = mean_into(y, 0, ma, ma_peer, None)
    m_out = mean_into(y, 3, mb, mb_peer, m_out)
    p_out = None
    for d in (0, 1, 3, 2):
        p_out = mean_into(y, d, p_own[d], after(a_peer[d], m_out), p_out)
    return (p_out[None], m_out[None])


def solution(mesh):
    return jax.shard_map(
        shards,
        mesh=mesh,
        in_specs=(
            P("replica", None, "fsdp", None),
            P("replica", None, "fsdp", None),
            P(None, "replica", None, "fsdp", None),
        ),
        out_specs=(P("replica", None, "fsdp", None), P("replica", None, "fsdp", None)),
        check_vma=False,
    )
```
